32 devices in a mesh: groups: 2 (over y), tensor: 2 (over core), fsdp: 8 (over z, x).
Axes of the slice: x: 2, y: 2, z: 4, core: 2. Of those that a mesh axis runs over, the one named last changes fastest.
Arguments:
- hidden: bfloat16 [4096, 1792], P(('groups', 'fsdp'), 'tensor'), parts along dimension 0, may hold values from -6 to 6
- grad_out: bfloat16 [4096, 4096], P(('groups', 'fsdp'), 'tensor'), parts along dimension 0, may hold values from -6 to 6
- tile_cols: int32 [14, 16], P('tensor'), may hold values from 0 to 31, as said below
- tile_owner: int32 [14, 16], P('tensor'), may hold values from 0 to 7, as said below
- tile_store: bfloat16 [2, 8, 21, 128, 128], P('tensor', 'fsdp'), may hold values from -0.1875 to 0.1875
Outputs:
- mixed_out: bfloat16 [4096, 4096], P(('groups', 'fsdp'), 'tensor'), parts along dimension 0
- grad_hidden: bfloat16 [4096, 1792], P(('groups', 'fsdp'), 'tensor'), parts along dimension 0
- tile_grads: float32 [4, 8, 21, 128, 128], P(('groups', 'tensor'), 'fsdp'), parts along dimension 0
The draws below stay inside these ranges and needn't reach their ends.
There are 2 independent parts, one for each index of `groups`. The reference program is written for one: setup_inputs(seed, part) draws one part's arguments, and reference() takes and returns one part's arrays. A program takes and returns all parts, laid end to end along the dimension named above; an argument that names none is the same for every part. Nothing has to cross between parts.
Inputs may be any that keep to these rules, and one draw needn't show every extreme that they name: `tile_cols`: each row holds 16 different column tile indices in increasing order. `tile_owner`: among the surviving tiles of each aligned block of 7 row tiles (the rows of one tensor index), no fsdp index owns more than 21, and one owns exactly 21.
All inputs are finite; a program needn't handle non-finite values.
Results may differ from the reference program's by a relative error of at most 0.0051.
Values may be sent and summed in bfloat16 or wider, within the bound.
A program may use at most 128 MiB of HBM per device.

```python
import jax
import jax.numpy as jnp
from jax import lax

TILE = 128
D_WIN = 4096
ROW_TILES_DEV = 7
TOK_DEV = 256
KEEP = 16
RT = 14
FF_WIN = 1792
TILES_DEV = 112
CAP = 21
TOKENS = 2048
N_TENSOR = 2
N_FSDP = 8


def draw_tile_cols(key, part):
    key = jax.random.fold_in(key, 11)
    row_keys = jax.random.split(key, RT)
    chosen = jax.vmap(lambda row_key: jax.random.permutation(row_key, 2 * KEEP)[:KEEP])(row_keys)
    return jnp.sort(chosen, axis=1).astype(jnp.int32)


def draw_tile_owner(key, part):
    key = jax.random.fold_in(key, 23)
    block_keys = jax.random.split(key, N_TENSOR)

    def draw_block(block_key):
        label_key, place_key = jax.random.split(block_key)
        labels = jax.random.permutation(label_key, N_FSDP).astype(jnp.int32)
        placing = jax.random.permutation(place_key, TILES_DEV)
        position = jnp.arange(TILES_DEV, dtype=jnp.int32)
        label_pick = jnp.where(position < CAP, 0, 1 + (position - CAP) % (N_FSDP - 1))
        assigned = labels[label_pick]
        return jnp.zeros((TILES_DEV,), jnp.int32).at[placing].set(assigned)
    return jax.vmap(draw_block)(block_keys).reshape(RT, KEEP).astype(jnp.int32)


def level_of(key, dims, cuts, least, largest):
    def one(dim, blocks):
        heights = jax.random.uniform(jax.random.fold_in(jax.random.fold_in(key, 6), dim), (blocks,), jnp.float32, least / len(cuts), largest / len(cuts))
        return jnp.repeat(jnp.exp(heights), dims[dim] // blocks).reshape((-1,) + (1,) * (len(dims) - dim - 1))

    factor_of = one(*cuts[0])
    for cut in cuts[1:]:
        factor_of = factor_of * one(*cut)
    return factor_of


def scatter_about(own_key, extent, scale, bound, cuts=(), kind=jnp.bfloat16):
    level = level_of(own_key, extent, cuts, -0.22, 0.18) if cuts else 1.0
    drawn = jax.random.normal(own_key, extent, jnp.float32) * scale * level
    return jnp.minimum(jnp.maximum(drawn, -bound), bound).astype(kind)


def setup_inputs(seed: int = 0, part: int = 0) -> dict:
    seeds = jax.random.split(jax.random.key(seed), 6)
    own_keys = jax.random.split(jax.random.fold_in(seeds[5], part), 6)
    return {
        "hidden": scatter_about(own_keys[0], (TOKENS, FF_WIN), 1.0, 6.0, ((0, 8), (1, 2))),
        "grad_out": scatter_about(own_keys[1], (TOKENS, D_WIN), 1.0, 6.0, ((0, 8), (1, 2))),
        "tile_cols": draw_tile_cols(jax.random.fold_in(seeds[5], 71), part),
        "tile_owner": draw_tile_owner(jax.random.fold_in(seeds[5], 71), part),
        "tile_store": scatter_about(seeds[4], (N_TENSOR, N_FSDP, CAP, TILE, TILE), (FF_WIN // 2) ** -0.5, 0.1875, ((0, 2), (1, 8))),
    }


def slot_tables(owners, owner_count, capacity):
    number = owners.shape[0]
    tile_ids = jnp.arange(number, dtype=jnp.int32)
    labels = jnp.arange(owner_count, dtype=jnp.int32)
    onehot = (owners[:, None] == labels[None, :]).astype(jnp.int32)
    ranking = jnp.sum((jnp.cumsum(onehot, axis=0) - 1) * onehot, axis=1).astype(jnp.int32)
    slot_index = jnp.arange(capacity, dtype=jnp.int32)
    matched = (owners[None, None, :] == labels[:, None, None]) & (ranking[None, None, :] == slot_index[None, :, None])
    slot_ids = jnp.sum(jnp.where(matched, tile_ids[None, None, :], 0), axis=2).astype(jnp.int32)
    filled = jnp.any(matched, axis=2)
    return ranking, slot_ids, filled


def block_terms(hid_block, grad_out, cols_block, owner_flat, store_block):
    highest = lax.Precision.HIGHEST
    ranking, slot_ids, filled = slot_tables(owner_flat, N_FSDP, CAP)
    weights = jnp.take(store_block, owner_flat * CAP + ranking, axis=0).reshape(ROW_TILES_DEV, KEEP, TILE, TILE).astype(jnp.float32)
    hid_tiles = hid_block.reshape(TOKENS, ROW_TILES_DEV, TILE).astype(jnp.float32)
    col_blocks = grad_out.reshape(TOKENS, 2 * KEEP, TILE)
    col_hot = (cols_block[:, :, None] == jnp.arange(2 * KEEP, dtype=jnp.int32)[None, None, :]).astype(jnp.float32)
    grad_scale = TOKENS ** -0.5
    partial_sum = jnp.zeros((TOKENS, 2 * KEEP, TILE), jnp.float32)
    input_parts = []
    weight_parts = []
    for row_tile in range(ROW_TILES_DEV):
        hid_row = hid_tiles[:, row_tile]
        product = jnp.einsum("ta,kab->tkb", hid_row, weights[row_tile], precision=highest)
        partial_sum = partial_sum + jnp.einsum("tkb,kc->tcb", product, col_hot[row_tile], precision=highest)
        chosen = jnp.take(col_blocks, cols_block[row_tile], axis=1).astype(jnp.float32)
        input_parts.append(jnp.einsum("tkb,kab->ta", chosen, weights[row_tile], precision=highest))
        local_term = jnp.einsum("fta,ftkb->fkab", hid_row.reshape(N_FSDP, TOK_DEV, TILE), chosen.reshape(N_FSDP, TOK_DEV, KEEP, TILE), precision=highest) * grad_scale
        rounded = lax.optimization_barrier(local_term.astype(jnp.bfloat16)).astype(jnp.float32)
        weight_parts.append(jnp.sum(rounded, axis=0))
    rounded_sum = lax.optimization_barrier(partial_sum.reshape(TOKENS, D_WIN).astype(jnp.bfloat16)).astype(jnp.float32)
    grad_hidden = jnp.concatenate(input_parts, axis=1).astype(jnp.bfloat16)
    pieces = jnp.concatenate(weight_parts, axis=0)
    owned_sum = jnp.take(pieces, slot_ids.reshape(-1), axis=0)
    owned_sum = jnp.where(filled.reshape(-1)[:, None, None], owned_sum, jnp.zeros_like(owned_sum))
    return rounded_sum, grad_hidden, owned_sum.reshape(N_FSDP, CAP, TILE, TILE)


def reference(hidden, grad_out, tile_cols, tile_owner, tile_store):
    def tensor_block(running, block_index):
        hid_start = (block_index * (ROW_TILES_DEV * TILE)).astype(jnp.int32)
        row_start = (block_index * ROW_TILES_DEV).astype(jnp.int32)
        hid_block = lax.dynamic_slice_in_dim(hidden, hid_start, ROW_TILES_DEV * TILE, 1)
        cols_block = lax.dynamic_slice_in_dim(tile_cols, row_start, ROW_TILES_DEV, 0)
        owner_flat = lax.dynamic_slice_in_dim(tile_owner, row_start, ROW_TILES_DEV, 0).reshape(-1)
        store_block = lax.dynamic_index_in_dim(tile_store, block_index, 0, keepdims=False).reshape(N_FSDP * CAP, TILE, TILE)
        rounded_sum, grad_hidden, owned_sum = block_terms(hid_block, grad_out, cols_block, owner_flat, store_block)
        return running + rounded_sum, (grad_hidden, owned_sum)

    blocks = jnp.arange(N_TENSOR, dtype=jnp.int32)
    summed, (hidden_grads, tile_grads) = lax.scan(tensor_block, jnp.zeros((TOKENS, D_WIN), jnp.float32), blocks)
    grad_hidden = jnp.moveaxis(hidden_grads, 0, 1).reshape(TOKENS, FF_WIN)
    return (summed.astype(jnp.bfloat16), grad_hidden, tile_grads)
```

```python
import functools

import jax
import jax.numpy as jnp
from jax import lax
from jax.experimental import pallas as pl
from jax.experimental.pallas import tpu as pltpu
from jax.sharding import PartitionSpec as P

MESH = pl.DeviceIdType.MESH


def index_tables(tile_cols, tile_owner, owner_count, capacity, col_tiles):
    row_tiles, keep = tile_cols.shape
    owners = tile_owner.reshape(-1)
    cols = tile_cols.reshape(-1)
    number = owners.shape[0]
    ids = jnp.arange(number, dtype=jnp.int32)
    earlier = (owners[:, None] == owners[None, :]) & (ids[None, :] < ids[:, None])
    rank = jnp.sum(earlier.astype(jnp.int32), axis=1)
    place = owners * capacity + rank
    slots = owner_count * capacity
    match = place[None, :] == jnp.arange(slots, dtype=jnp.int32)[:, None]
    slot_row = row_tiles + jnp.sum(
        jnp.where(match, ids[None, :] // keep - row_tiles, 0), axis=1)
    slot_col = jnp.sum(jnp.where(match, cols[None, :], 0), axis=1)
    hot = tile_cols[:, :, None] == jnp.arange(col_tiles, dtype=jnp.int32)[None, None, :]
    dense = slots + jnp.sum(
        jnp.where(hot, place.reshape(row_tiles, keep)[:, :, None] - slots, 0), axis=1)
    return jnp.concatenate([slot_row, slot_col, dense.reshape(-1)])


def kernel(cfg, tab, hid_ref, grad_ref, store_ref, mixed_ref, gh_ref, tg_ref,
           hid_t, gbuf, wbuf, pbuf, xrecv, zrecv, block, gh_acc, psend, pown, precv,
           g_sem, ax_sem, ar_sem, al_sem, yx_sem, yr_sem, yl_sem,
           rx_sem, rz_send, rz_recv, p_sem):
    lines, capacity, row_tiles, col_tiles, width, scale, paired = cfg
    owners = 2 * lines
    slots = owners * capacity
    half = width // 2
    last = lines - 1
    me = lax.axis_index("fsdp")
    group = lax.axis_index("groups")
    core = lax.axis_index("tensor")
    z, x = me // 2, lax.rem(me, 2)
    x_dev = {"fsdp": z * 2 + 1 - x}
    y_dev = {"groups": 1 - group}
    up_dev = {"fsdp": me + 2}
    down_dev = {"fsdp": me - 2}
    core_dev = {"tensor": 1 - core}
    own_tiles = grad_ref.shape[1] // width

    barrier = pltpu.get_barrier_semaphore()

    def greet(device):
        pl.semaphore_signal(barrier, inc=1, device_id=device, device_id_type=MESH)

    greet(x_dev)
    greet(y_dev)
    if paired:
        greet(core_dev)

    @pl.when(z < last)
    def _():
        greet(up_dev)

    @pl.when(z > 0)
    def _():
        greet(down_dev)

    for h in range(2):
        wbuf[h, pl.ds(me * capacity, capacity)] = store_ref[:, h * half:(h + 1) * half, :]
        wbuf[h, slots] = jnp.zeros((half, width), wbuf.dtype)
    first = core * own_tiles if paired else 0
    for c in range(own_tiles):
        gbuf[first + c] = grad_ref[:, c * width:(c + 1) * width]

    peers = (3 if paired else 2) + jnp.where(z < last, 1, 0) + jnp.where(z > 0, 1, 0)
    pl.semaphore_wait(barrier, peers)

    sent = []

    def copy(src, dst, send, recv, device):
        return pltpu.make_async_remote_copy(
            src_ref=src, dst_ref=dst, send_sem=send, recv_sem=recv,
            device_id=device, device_id_type=MESH)

    def start(cond, desc):
        if cond is None:
            desc.start()
        else:
            @pl.when(cond)
            def _():
                desc.start()
        sent.append((cond, desc))

    def wait_recv(cond, desc):
        if cond is None:
            desc.wait_recv()
        else:
            @pl.when(cond)
            def _():
                desc.wait_recv()

    def chunk(owner):
        return wbuf.at[group, pl.ds(owner * capacity, capacity)]

    def other_chunk(owner):
        return wbuf.at[1 - group, pl.ds(owner * capacity, capacity)]

    def pick(b):
        return x if b == 0 else 1 - x

    def up_send(j, b):
        part = chunk((z - j) * 2 + pick(b))
        return ((z < last) & (z >= j),
                copy(part, part, ar_sem.at[0, j, b], ar_sem.at[1, j, b], up_dev))

    def up_recv(j, b):
        part = chunk((z - 1 - j) * 2 + pick(b))
        return (z >= j + 1, copy(part, part, ar_sem.at[0, j, b], ar_sem.at[1, j, b], up_dev))

    def down_send(j, b):
        part = chunk((z + j) * 2 + pick(b))
        return ((z > 0) & (z + j <= last),
                copy(part, part, al_sem.at[0, j, b], al_sem.at[1, j, b], down_dev))

    def down_recv(j, b):
        part = chunk((z + 1 + j) * 2 + pick(b))
        return (z + 1 + j <= last,
                copy(part, part, al_sem.at[0, j, b], al_sem.at[1, j, b], down_dev))

    def y_up(j, b, part):
        piece = part((z - 1 - j) * 2 + pick(b))
        return (z >= j + 1, copy(piece, piece, yr_sem.at[0, j, b], yr_sem.at[1, j, b], y_dev))

    def y_down(j, b, part):
        piece = part((z + 1 + j) * 2 + pick(b))
        return (z + 1 + j <= last,
                copy(piece, piece, yl_sem.at[0, j, b], yl_sem.at[1, j, b], y_dev))

    def y_x(part):
        piece = part(z * 2 + 1 - x)
        return (None, copy(piece, piece, yx_sem.at[0], yx_sem.at[1], y_dev))

    if paired:
        piece = gbuf.at[pl.ds(core * own_tiles, own_tiles)]
        there = gbuf.at[pl.ds((1 - core) * own_tiles, own_tiles)]
        g_copy = copy(piece, piece, g_sem.at[0], g_sem.at[1], core_dev)
        start(None, g_copy)
    start(None, copy(chunk(me), chunk(me), ax_sem.at[0], ax_sem.at[1], x_dev))
    start(*up_send(0, 0))
    start(*down_send(0, 0))

    for r in range(row_tiles):
        hid_t[r] = hid_ref[:, r * width:(r + 1) * width].T
    hid_t[row_tiles] = jnp.zeros(hid_t.shape[1:], hid_t.dtype)

    if paired:
        copy(there, there, g_sem.at[0], g_sem.at[1], core_dev).wait_recv()

    def pieces(owner):
        def body(s, carry):
            at = owner * capacity + s
            left = hid_t[tab[at]]
            right = gbuf[tab[slots + at]]
            term = jnp.dot(left, right, preferred_element_type=jnp.float32)
            pbuf[at] = (term * scale).astype(pbuf.dtype)
            return carry
        lax.fori_loop(0, capacity, body, 0, unroll=3)

    def shard(owner):
        return pbuf.at[pl.ds(owner * capacity, capacity)]

    def target(k):
        value = jnp.int32(0)
        for at in range(lines):
            order = sorted(range(lines), key=lambda t: -abs(t - at))
            value = jnp.where(z == at, order[k], value)
        return value

    def gather_x():
        part = chunk(z * 2 + 1 - x)
        copy(part, part, ax_sem.at[0], ax_sem.at[1], x_dev).wait_recv()
        start(*up_send(0, 1))
        start(*down_send(0, 1))
        start(*y_x(chunk))

    def gather_z(j, b):
        wait_recv(*up_recv(j, b))
        if j + 1 < last:
            start(*up_send(j + 1, b))
        start(*y_up(j, b, chunk))
        wait_recv(*down_recv(j, b))
        if j + 1 < last:
            start(*down_send(j + 1, b))
        start(*y_down(j, b, chunk))

    steps = [gather_x]
    for j in range(last):
        for b in range(2):
            steps.append(functools.partial(gather_z, j, b))
    steps = iter(steps)

    def gather_step():
        step = next(steps, None)
        if step is not None:
            step()

    targets = [target(k) for k in range(lines)]
    for k in range(lines):
        owner = targets[k] * 2 + 1 - x
        pieces(owner)
        start(None, copy(shard(owner), xrecv.at[k], rx_sem.at[0, k], rx_sem.at[1, k], x_dev))
    gather_step()
    for k in range(lines):
        pieces(targets[k] * 2 + x)
        if k >= lines - 2:
            gather_step()

    def add_up(k):
        goal = targets[k]
        base = (goal * 2 + x) * capacity
        copy(xrecv.at[k], xrecv.at[k], rx_sem.at[0, k], rx_sem.at[1, k], x_dev).wait_recv()
        through = ((goal > z) & (z > 0)) | ((goal < z) & (z < last))

        @pl.when(through)
        def _():
            copy(zrecv.at[goal], zrecv.at[goal], rz_send.at[k], rz_recv.at[goal],
                 x_dev).wait_recv()

            def body(s, carry):
                total = (pbuf[base + s].astype(jnp.float32) + xrecv[k, s].astype(jnp.float32)
                         + zrecv[goal, s].astype(jnp.float32))
                pbuf[base + s] = total.astype(pbuf.dtype)
                return carry
            lax.fori_loop(0, capacity, body, 0)

        @pl.when(jnp.logical_not(through))
        def _():
            def body(s, carry):
                total = pbuf[base + s].astype(jnp.float32) + xrecv[k, s].astype(jnp.float32)
                pbuf[base + s] = total.astype(pbuf.dtype)
                return carry
            lax.fori_loop(0, capacity, body, 0)

        source = pbuf.at[pl.ds(base, capacity)]
        start(goal > z, copy(source, zrecv.at[goal], rz_send.at[k], rz_recv.at[goal], up_dev))
        land = jnp.where(goal == z - 1, lines, goal)
        start(goal < z, copy(source, zrecv.at[land], rz_send.at[k], rz_recv.at[land], down_dev))

    def finish():
        k = last
        base = me * capacity
        copy(xrecv.at[k], xrecv.at[k], rx_sem.at[0, k], rx_sem.at[1, k], x_dev).wait_recv()

        def body(s, carry):
            tg_ref[s] = pbuf[base + s].astype(jnp.float32) + xrecv[k, s].astype(jnp.float32)
            return carry
        lax.fori_loop(0, capacity, body, 0)

        for cond, slot in ((z > 0, z), (z < last, lines)):
            @pl.when(cond)
            def _():
                copy(zrecv.at[slot], zrecv.at[slot], rz_send.at[k], rz_recv.at[slot],
                     x_dev).wait_recv()

                def more(s, carry):
                    tg_ref[s] = tg_ref[s] + zrecv[slot, s].astype(jnp.float32)
                    return carry
                lax.fori_loop(0, capacity, more, 0)

    for k in range(last):
        gather_step()
        add_up(k)
        gather_step()
    for step in steps:
        step()

    wait_recv(*y_x(other_chunk))
    for j in range(last):
        for b in range(2):
            wait_recv(*y_up(j, b, other_chunk))
            wait_recv(*y_down(j, b, other_chunk))

    gh_acc[...] = jnp.zeros_like(gh_acc)

    def products(c0):
        for r in range(row_tiles):
            for q in range(2):
                at = tab[2 * slots + r * col_tiles + c0 + q]
                for h in range(2):
                    block[r * width + h * half:r * width + (h + 1) * half,
                          q * width:(q + 1) * width] = wbuf[h, at]
        dense = block[...]
        cot = jnp.concatenate([gbuf[c0], gbuf[c0 + 1]], axis=1)
        gh_acc[...] += lax.dot_general(cot, dense, (((1,), (1,)), ((), ())),
                                       preferred_element_type=jnp.float32)
        out = jnp.dot(hid_ref[...], dense, preferred_element_type=jnp.float32)
        return out.astype(jnp.bfloat16)

    pairs = own_tiles // 2
    if paired:
        def partial_copy(i):
            return copy(psend.at[i], precv.at[i], p_sem.at[0, i], p_sem.at[1, i], core_dev)

        def away(i, carry):
            psend[i] = products((1 - core) * own_tiles + 2 * i)
            partial_copy(i).start()
            return carry
        lax.fori_loop(0, pairs, away, 0)

        def home(i, carry):
            pown[i] = products(core * own_tiles + 2 * i)
            return carry
        lax.fori_loop(0, pairs, home, 0)
        gh_ref[...] = gh_acc[...].astype(gh_ref.dtype)
        for i in range(pairs):
            partial_copy(i).wait()
            mixed_ref[:, 2 * i * width:2 * (i + 1) * width] = (
                pown[i].astype(jnp.float32) + precv[i].astype(jnp.float32)
            ).astype(mixed_ref.dtype)
    else:
        for i in range(pairs):
            mixed_ref[:, 2 * i * width:2 * (i + 1) * width] = products(2 * i)
        gh_ref[...] = gh_acc[...].astype(gh_ref.dtype)

    finish()
    for cond, desc in sent:
        if cond is None:
            desc.wait_send()
        else:
            pl.when(cond)(desc.wait_send)


def shards(hidden, grad_out, tile_cols, tile_owner, tile_store):
    owners = lax.axis_size("fsdp")
    paired = lax.axis_size("tensor") == 2
    tokens = hidden.shape[0]
    row_tiles, keep = tile_cols.shape
    capacity, width = tile_store.shape[2:4]
    col_tiles = 2 * keep
    lines = owners // 2
    half = width // 2
    slots = owners * capacity
    scale = float(tokens * owners) ** (-0.5)
    tables = index_tables(tile_cols, tile_owner, owners, capacity, col_tiles)
    if not paired:
        grad_out = lax.all_gather(grad_out, "tensor", axis=1, tiled=True)
    store = tile_store.reshape(capacity, width, width)
    hops = lines - 1
    pairs = grad_out.shape[1] // width // 2
    few = pairs if paired else 1
    bf16, f32 = jnp.bfloat16, jnp.float32
    dma = pltpu.SemaphoreType.DMA
    vmem = pl.BlockSpec(memory_space=pltpu.VMEM)
    cfg = (lines, capacity, row_tiles, col_tiles, width, scale, paired)
    mixed, gh, tg = pl.pallas_call(
        functools.partial(kernel, cfg),
        out_shape=(
            jax.ShapeDtypeStruct(grad_out.shape, bf16),
            jax.ShapeDtypeStruct(hidden.shape, bf16),
            jax.ShapeDtypeStruct((capacity, width, width), f32),
        ),
        in_specs=[pl.BlockSpec(memory_space=pltpu.SMEM)] + [vmem] * 3,
        out_specs=(vmem,) * 3,
        scratch_shapes=[
            pltpu.VMEM((row_tiles + 1, width, tokens), bf16),
            pltpu.VMEM((col_tiles, tokens, width), bf16),
            pltpu.VMEM((2, slots + 1, half, width), bf16),
            pltpu.VMEM((slots, width, width), bf16),
            pltpu.VMEM((lines, capacity, width, width), bf16),
            pltpu.VMEM((lines + 1, capacity, width, width), bf16),
            pltpu.VMEM((row_tiles * width, 2 * width), bf16),
            pltpu.VMEM(hidden.shape, f32),
            pltpu.VMEM((few, tokens, 2 * width), bf16),
            pltpu.VMEM((few, tokens, 2 * width), bf16),
            pltpu.VMEM((few, tokens, 2 * width), bf16),
            dma((2,)), dma((2,)), dma((2, hops, 2)), dma((2, hops, 2)),
            dma((2,)), dma((2, hops, 2)), dma((2, hops, 2)),
            dma((2, lines)), dma((lines,)), dma((lines + 1,)), dma((2, few)),
        ],
        compiler_params=pltpu.CompilerParams(
            collective_id=0, has_side_effects=True, vmem_limit_bytes=48 * 1024 * 1024),
    )(tables, hidden, grad_out, store)
    if not paired:
        mixed = lax.psum_scatter(mixed, "tensor", scatter_dimension=1, tiled=True)
    return mixed, gh, tg.reshape(1, 1, capacity, width, width)


def solution(mesh):
    placed = (
        P(("groups", "fsdp"), "tensor"),
        P(("groups", "fsdp"), "tensor"),
        P("tensor", None),
        P("tensor", None),
        P("tensor", "fsdp", None, None, None),
    )
    return jax.shard_map(
        shards,
        mesh=mesh,
        in_specs=placed,
        out_specs=(
            P(("groups", "fsdp"), "tensor"),
            P(("groups", "fsdp"), "tensor"),
            P(("groups", "tensor"), "fsdp", None, None, None),
        ),
        check_vma=False,
    )
```

```python
import functools

import jax
import jax.numpy as jnp
from jax import lax
from jax.experimental import pallas as pl
from jax.experimental.pallas import tpu as pltpu
from jax.sharding import PartitionSpec as P

MESH = pl.DeviceIdType.MESH


def index_tables(tile_cols, tile_owner, owner_count, capacity, col_tiles):
    row_tiles, keep = tile_cols.shape
    owners = tile_owner.reshape(-1)
    cols = tile_cols.reshape(-1)
    number = owners.shape[0]
    ids = jnp.arange(number, dtype=jnp.int32)
    earlier = (owners[:, None] == owners[None, :]) & (ids[None, :] < ids[:, None])
    rank = jnp.sum(earlier.astype(jnp.int32), axis=1)
    place = owners * capacity + rank
    slots = owner_count * capacity
    match = place[None, :] == jnp.arange(slots, dtype=jnp.int32)[:, None]
    zero_tile = row_tiles * col_tiles
    tile = ids // keep * col_tiles + cols
    slot_tile = zero_tile + jnp.sum(jnp.where(match, tile[None, :] - zero_tile, 0), axis=1)
    hot = tile_cols[:, :, None] == jnp.arange(col_tiles, dtype=jnp.int32)[None, None, :]
    dense = slots + jnp.sum(
        jnp.where(hot, place.reshape(row_tiles, keep)[:, :, None] - slots, 0), axis=1)
    return jnp.concatenate([slot_tile, dense.reshape(-1)])


def kernel(cfg, tab, hid_hbm, grad_hbm, store_hbm, mixed_ref, gh_ref, tg_ref,
           hid, hid_t, gfull, wbuf, dmat, pbuf, xrecv, zrecv, block, gh_acc,
           psend, pown, precv, in_sem,
           g_sem, ax_sem, ar_sem, al_sem, yx_sem, yr_sem, yl_sem,
           rx_sem, rz_send, rz_recv, p_sem):
    lines, capacity, row_tiles, col_tiles, width, scale, paired, subs = cfg
    owners = 2 * lines
    slots = owners * capacity
    half = width // 2
    last = lines - 1
    me = lax.axis_index("fsdp")
    group = lax.axis_index("groups")
    core = lax.axis_index("tensor")
    z, x = me // 2, lax.rem(me, 2)
    x_dev = {"fsdp": z * 2 + 1 - x}
    y_dev = {"groups": 1 - group}
    up_dev = {"fsdp": me + 2}
    down_dev = {"fsdp": me - 2}
    core_dev = {"tensor": 1 - core}
    own_tiles = grad_hbm.shape[1] // width
    part = capacity // subs
    first = core if paired else 0

    own_rows = pl.ds(me * capacity, capacity)
    hid_in = pltpu.make_async_copy(hid_hbm, hid, in_sem.at[0])
    grad_in = pltpu.make_async_copy(grad_hbm, gfull.at[first], in_sem.at[1])
    store_in = [pltpu.make_async_copy(store_hbm.at[:, h * half:(h + 1) * half, :],
                                      wbuf.at[h, own_rows], in_sem.at[2 + h])
                for h in range(2)]
    hid_in.start()
    grad_in.start()
    barrier = pltpu.get_barrier_semaphore()

    def greet(device):
        pl.semaphore_signal(barrier, inc=1, device_id=device, device_id_type=MESH)

    greet(x_dev)
    greet(y_dev)
    if paired:
        greet(core_dev)

    @pl.when(z < last)
    def _():
        greet(up_dev)

    @pl.when(z > 0)
    def _():
        greet(down_dev)

    for h in range(2):
        wbuf[h, slots] = jnp.zeros((half, width), wbuf.dtype)
    dmat[row_tiles * col_tiles] = jnp.zeros((width, width), dmat.dtype)

    peers = (3 if paired else 2) + jnp.where(z < last, 1, 0) + jnp.where(z > 0, 1, 0)
    pl.semaphore_wait(barrier, peers)

    sent = []

    def copy(src, dst, send, recv, device):
        return pltpu.make_async_remote_copy(
            src_ref=src, dst_ref=dst, send_sem=send, recv_sem=recv,
            device_id=device, device_id_type=MESH)

    def start(cond, desc):
        if cond is None:
            desc.start()
        else:
            @pl.when(cond)
            def _():
                desc.start()
        sent.append((cond, desc))

    def wait_recv(cond, desc):
        if cond is None:
            desc.wait_recv()
        else:
            @pl.when(cond)
            def _():
                desc.wait_recv()

    def chunk(owner):
        return wbuf.at[group, pl.ds(owner * capacity, capacity)]

    def other_chunk(owner):
        return wbuf.at[1 - group, pl.ds(owner * capacity, capacity)]

    def pick(b):
        return x if b == 0 else 1 - x

    def up_send(j, b):
        part = chunk((z - j) * 2 + pick(b))
        return ((z < last) & (z >= j),
                copy(part, part, ar_sem.at[0, j, b], ar_sem.at[1, j, b], up_dev))

    def up_recv(j, b):
        part = chunk((z - 1 - j) * 2 + pick(b))
        return (z >= j + 1, copy(part, part, ar_sem.at[0, j, b], ar_sem.at[1, j, b], up_dev))

    def down_send(j, b):
        part = chunk((z + j) * 2 + pick(b))
        return ((z > 0) & (z + j <= last),
                copy(part, part, al_sem.at[0, j, b], al_sem.at[1, j, b], down_dev))

    def down_recv(j, b):
        part = chunk((z + 1 + j) * 2 + pick(b))
        return (z + 1 + j <= last,
                copy(part, part, al_sem.at[0, j, b], al_sem.at[1, j, b], down_dev))

    def y_up(j, b, part):
        piece = part((z - 1 - j) * 2 + pick(b))
        return (z >= j + 1, copy(piece, piece, yr_sem.at[0, j, b], yr_sem.at[1, j, b], y_dev))

    def y_down(j, b, part):
        piece = part((z + 1 + j) * 2 + pick(b))
        return (z + 1 + j <= last,
                copy(piece, piece, yl_sem.at[0, j, b], yl_sem.at[1, j, b], y_dev))

    def y_x(part):
        piece = part(z * 2 + 1 - x)
        return (None, copy(piece, piece, yx_sem.at[0], yx_sem.at[1], y_dev))

    mine = store_hbm.at[:, pl.ds(pl.multiple_of(group * half, half), half), :]

    def from_store(cond, sems, device):
        start(cond, copy(mine, chunk(me), sems[0], sems[1], device))

    from_store(None, (ax_sem.at[0], ax_sem.at[1]), x_dev)
    if paired:
        start(None, copy(grad_hbm, gfull.at[core], g_sem.at[0], g_sem.at[1], core_dev))
    from_store(z < last, (ar_sem.at[0, 0, 0], ar_sem.at[1, 0, 0]), up_dev)
    from_store(z > 0, (al_sem.at[0, 0, 0], al_sem.at[1, 0, 0]), down_dev)
    for desc in store_in:
        desc.start()

    hid_in.wait()
    for r in range(row_tiles):
        hid_t[r * width:(r + 1) * width] = hid[:, r * width:(r + 1) * width].T

    pairs = own_tiles // 2

    def columns(side, i):
        return gfull[side, :, pl.ds(pl.multiple_of(2 * i * width, 2 * width), 2 * width)]

    def gradients(side):
        def body(i, carry):
            term = jnp.dot(hid_t[...], columns(side, i), preferred_element_type=jnp.float32)
            term = (term * scale).astype(dmat.dtype)
            at = side * own_tiles + 2 * i
            for r in range(row_tiles):
                for q in range(2):
                    dmat[r * col_tiles + at + q] = term[r * width:(r + 1) * width,
                                                        q * width:(q + 1) * width]
            return carry
        lax.fori_loop(0, pairs, body, 0)

    grad_in.wait()
    gradients(first)
    if paired:
        there = gfull.at[1 - core]
        copy(there, there, g_sem.at[0], g_sem.at[1], core_dev).wait_recv()
        gradients(1 - core)

    def pieces(owner, sub):
        base = owner * capacity + sub * part

        def body(s, carry):
            pbuf[base + s] = dmat[tab[base + s]]
            return carry
        lax.fori_loop(0, part, body, 0, unroll=True)

    def shard(owner, sub):
        return pbuf.at[pl.ds(owner * capacity + sub * part, part)]

    def target(k):
        value = jnp.int32(0)
        for at in range(lines):
            order = sorted(range(lines), key=lambda t: -abs(t - at))
            value = jnp.where(z == at, order[k], value)
        return value

    def gather_x():
        part = chunk(z * 2 + 1 - x)
        copy(part, part, ax_sem.at[0], ax_sem.at[1], x_dev).wait_recv()
        start(*up_send(0, 1))
        start(*down_send(0, 1))
        start(*y_x(chunk))

    def gather_z(j, b):
        wait_recv(*up_recv(j, b))
        if j + 1 < last:
            start(*up_send(j + 1, b))
        start(*y_up(j, b, chunk))
        wait_recv(*down_recv(j, b))
        if j + 1 < last:
            start(*down_send(j + 1, b))
        start(*y_down(j, b, chunk))

    steps = [gather_x]
    for j in range(last):
        for b in range(2):
            steps.append(functools.partial(gather_z, j, b))
    steps = iter(steps)

    def gather_step():
        step = next(steps, None)
        if step is not None:
            step()

    targets = [target(k) for k in range(lines)]

    def x_copy(k, sub):
        owner = targets[k] * 2 + 1 - x
        i = k * subs + sub
        return copy(shard(owner, sub), xrecv.at[i], rx_sem.at[0, i], rx_sem.at[1, i], x_dev)

    for k in range(lines):
        for sub in range(subs):
            pieces(targets[k] * 2 + 1 - x, sub)
            start(None, x_copy(k, sub))
        if k == 0:
            gather_step()
    for k in range(lines):
        for sub in range(subs):
            pieces(targets[k] * 2 + x, sub)
        if k == 0:
            gather_step()

    def arrived(slot, k, sub):
        copy(zrecv.at[slot, sub], zrecv.at[slot, sub], rz_send.at[k, sub],
             rz_recv.at[slot, sub], x_dev).wait_recv()

    def add_up(k, sub):
        goal = targets[k]
        i = k * subs + sub
        base = (goal * 2 + x) * capacity + sub * part
        x_copy(k, sub).wait_recv()
        through = ((goal > z) & (z > 0)) | ((goal < z) & (z < last))

        @pl.when(through)
        def _():
            arrived(goal, k, sub)

            def body(s, carry):
                total = (pbuf[base + s].astype(jnp.float32) + xrecv[i, s].astype(jnp.float32)
                         + zrecv[goal, sub, s].astype(jnp.float32))
                pbuf[base + s] = total.astype(pbuf.dtype)
                return carry
            lax.fori_loop(0, part, body, 0)

        @pl.when(jnp.logical_not(through))
        def _():
            def body(s, carry):
                total = pbuf[base + s].astype(jnp.float32) + xrecv[i, s].astype(jnp.float32)
                pbuf[base + s] = total.astype(pbuf.dtype)
                return carry
            lax.fori_loop(0, part, body, 0)

        source = pbuf.at[pl.ds(base, part)]
        land = jnp.where(goal == z - 1, lines, goal)
        start(goal > z, copy(source, zrecv.at[goal, sub], rz_send.at[k, sub],
                             rz_recv.at[goal, sub], up_dev))
        start(goal < z, copy(source, zrecv.at[land, sub], rz_send.at[k, sub],
                             rz_recv.at[land, sub], down_dev))

    def finish(sub):
        k = last
        i = k * subs + sub
        base = me * capacity + sub * part
        x_copy(k, sub).wait_recv()

        def body(s, carry):
            tg_ref[sub * part + s] = (pbuf[base + s].astype(jnp.float32)
                                      + xrecv[i, s].astype(jnp.float32))
            return carry
        lax.fori_loop(0, part, body, 0)

        for cond, slot in ((z > 0, z), (z < last, lines)):
            @pl.when(cond)
            def _():
                arrived(slot, k, sub)

                def more(s, carry):
                    at = sub * part + s
                    tg_ref[at] = tg_ref[at] + zrecv[slot, sub, s].astype(jnp.float32)
                    return carry
                lax.fori_loop(0, part, more, 0)

    for k in range(last):
        for sub in range(subs):
            add_up(k, sub)
            if sub % 2 == 0:
                gather_step()
    for step in steps:
        step()

    for desc in store_in:
        desc.wait()
    wait_recv(*y_x(other_chunk))
    for j in range(last):
        for b in range(2):
            wait_recv(*y_up(j, b, other_chunk))
            wait_recv(*y_down(j, b, other_chunk))

    gh_acc[...] = jnp.zeros_like(gh_acc)

    def products(side, i):
        c0 = side * own_tiles + 2 * i
        for r in range(row_tiles):
            for q in range(2):
                at = tab[slots + r * col_tiles + c0 + q]
                for h in range(2):
                    block[r * width + h * half:r * width + (h + 1) * half,
                          q * width:(q + 1) * width] = wbuf[h, at]
        dense = block[...]
        cot = columns(side, i)
        gh_acc[...] += lax.dot_general(cot, dense, (((1,), (1,)), ((), ())),
                                       preferred_element_type=jnp.float32)
        out = jnp.dot(hid[...], dense, preferred_element_type=jnp.float32)
        return out.astype(jnp.bfloat16)

    if paired:
        def partial_copy(i):
            return copy(psend.at[i], precv.at[i], p_sem.at[0, i], p_sem.at[1, i], core_dev)

        def away(i, carry):
            psend[i] = products(1 - core, i)
            partial_copy(i).start()
            return carry
        lax.fori_loop(0, pairs, away, 0)

        def home(i, carry):
            pown[i] = products(core, i)
            return carry
        lax.fori_loop(0, pairs, home, 0)
        gh_ref[...] = gh_acc[...].astype(gh_ref.dtype)
        for i in range(pairs):
            partial_copy(i).wait()
            mixed_ref[:, 2 * i * width:2 * (i + 1) * width] = (
                pown[i].astype(jnp.float32) + precv[i].astype(jnp.float32)
            ).astype(mixed_ref.dtype)
    else:
        for i in range(pairs):
            mixed_ref[:, 2 * i * width:2 * (i + 1) * width] = products(0, i)
        gh_ref[...] = gh_acc[...].astype(gh_ref.dtype)

    for sub in range(subs):
        finish(sub)
    for cond, desc in sent:
        if cond is None:
            desc.wait_send()
        else:
            pl.when(cond)(desc.wait_send)


def shards(hidden, grad_out, tile_cols, tile_owner, tile_store):
    owners = lax.axis_size("fsdp")
    paired = lax.axis_size("tensor") == 2
    tokens = hidden.shape[0]
    row_tiles, keep = tile_cols.shape
    capacity, width = tile_store.shape[2:4]
    col_tiles = 2 * keep
    lines = owners // 2
    half = width // 2
    slots = owners * capacity
    scale = float(tokens * owners) ** (-0.5)
    tables = index_tables(tile_cols, tile_owner, owners, capacity, col_tiles)
    if not paired:
        grad_out = lax.all_gather(grad_out, "tensor", axis=1, tiled=True)
    store = tile_store.reshape(capacity, width, width)
    hops = lines - 1
    pairs = grad_out.shape[1] // width // 2
    subs = 3 if capacity % 3 == 0 else 1
    part = capacity // subs
    sides = 2 if paired else 1
    few = pairs if paired else 1
    bf16, f32 = jnp.bfloat16, jnp.float32
    dma = pltpu.SemaphoreType.DMA
    vmem = pl.BlockSpec(memory_space=pltpu.VMEM)
    cfg = (lines, capacity, row_tiles, col_tiles, width, scale, paired, subs)
    mixed, gh, tg = pl.pallas_call(
        functools.partial(kernel, cfg),
        out_shape=(
            jax.ShapeDtypeStruct(grad_out.shape, bf16),
            jax.ShapeDtypeStruct(hidden.shape, bf16),
            jax.ShapeDtypeStruct((capacity, width, width), f32),
        ),
        in_specs=[pl.BlockSpec(memory_space=pltpu.SMEM)] + [pl.BlockSpec(memory_space=pl.ANY)] * 3,
        out_specs=(vmem,) * 3,
        scratch_shapes=[
            pltpu.VMEM(hidden.shape, bf16),
            pltpu.VMEM((row_tiles * width, tokens), bf16),
            pltpu.VMEM((sides,) + grad_out.shape, bf16),
            pltpu.VMEM((2, slots + 1, half, width), bf16),
            pltpu.VMEM((row_tiles * col_tiles + 1, width, width), bf16),
            pltpu.VMEM((slots, width, width), bf16),
            pltpu.VMEM((lines * subs, part, width, width), bf16),
            pltpu.VMEM((lines + 1, subs, part, width, width), bf16),
            pltpu.VMEM((row_tiles * width, 2 * width), bf16),
            pltpu.VMEM(hidden.shape, f32),
            pltpu.VMEM((few, tokens, 2 * width), bf16),
            pltpu.VMEM((few, tokens, 2 * width), bf16),
            pltpu.VMEM((few, tokens, 2 * width), bf16),
            dma((4,)), dma((2,)), dma((2,)), dma((2, hops, 2)), dma((2, hops, 2)),
            dma((2,)), dma((2, hops, 2)), dma((2, hops, 2)),
            dma((2, lines * subs)), dma((lines, subs)), dma((lines + 1, subs)), dma((2, few)),
        ],
        compiler_params=pltpu.CompilerParams(
            collective_id=0, has_side_effects=True, vmem_limit_bytes=56 * 1024 * 1024),
    )(tables, hidden, grad_out, store)
    if not paired:
        mixed = lax.psum_scatter(mixed, "tensor", scatter_dimension=1, tiled=True)
    return mixed, gh, tg.reshape(1, 1, capacity, width, width)


def solution(mesh):
    placed = (
        P(("groups", "fsdp"), "tensor"),
        P(("groups", "fsdp"), "tensor"),
        P("tensor", None),
        P("tensor", None),
        P("tensor", "fsdp", None, None, None),
    )
    return jax.shard_map(
        shards,
        mesh=mesh,
        in_specs=placed,
        out_specs=(
            P(("groups", "fsdp"), "tensor"),
            P(("groups", "fsdp"), "tensor"),
            P(("groups", "tensor"), "fsdp", None, None, None),
        ),
        check_vma=False,
    )
```

```python
import functools

import jax
import jax.numpy as jnp
from jax import lax
from jax.experimental import pallas as pl
from jax.experimental.pallas import tpu as pltpu
from jax.sharding import PartitionSpec as P

MESH = pl.DeviceIdType.MESH


def index_tables(tile_cols, tile_owner, owner_count, capacity, col_tiles):
    row_tiles, keep = tile_cols.shape
    owners = tile_owner.reshape(-1)
    cols = tile_cols.reshape(-1)
    number = owners.shape[0]
    ids = jnp.arange(number, dtype=jnp.int32)
    earlier = (owners[:, None] == owners[None, :]) & (ids[None, :] < ids[:, None])
    rank = jnp.sum(earlier.astype(jnp.int32), axis=1)
    place = owners * capacity + rank
    slots = owner_count * capacity
    match = place[None, :] == jnp.arange(slots, dtype=jnp.int32)[:, None]
    zero_tile = row_tiles * col_tiles
    tile = ids // keep * col_tiles + cols
    slot_tile = zero_tile + jnp.sum(jnp.where(match, tile[None, :] - zero_tile, 0), axis=1)
    hot = tile_cols[:, :, None] == jnp.arange(col_tiles, dtype=jnp.int32)[None, None, :]
    dense = slots + jnp.sum(
        jnp.where(hot, place.reshape(row_tiles, keep)[:, :, None] - slots, 0), axis=1)
    return jnp.concatenate([slot_tile, dense.reshape(-1)])


def kernel(cfg, tab, hid_hbm, grad_hbm, store_hbm, mixed_ref, gh_ref, tg_ref,
           hid, hid_t, gfull, wbuf, dmat, pbuf, xrecv, zrecv, block, gh_acc,
           psend, pown, precv, in_sem,
           g_sem, ax_sem, ar_sem, al_sem, yx_sem, yr_sem, yl_sem,
           rx_sem, rz_send, rz_recv, p_sem):
    lines, capacity, row_tiles, col_tiles, width, scale, paired, subs = cfg
    owners = 2 * lines
    slots = owners * capacity
    half = width // 2
    last = lines - 1
    me = lax.axis_index("fsdp")
    group = lax.axis_index("groups")
    core = lax.axis_index("tensor")
    z, x = me // 2, lax.rem(me, 2)
    x_dev = {"fsdp": z * 2 + 1 - x}
    y_dev = {"groups": 1 - group}
    up_dev = {"fsdp": me + 2}
    down_dev = {"fsdp": me - 2}
    core_dev = {"tensor": 1 - core}
    own_tiles = grad_hbm.shape[1] // width
    part = capacity // subs
    first = core if paired else 0

    own_rows = pl.ds(me * capacity, capacity)
    hid_in = pltpu.make_async_copy(hid_hbm, hid, in_sem.at[0])
    grad_in = pltpu.make_async_copy(grad_hbm, gfull.at[first], in_sem.at[1])
    store_in = [pltpu.make_async_copy(store_hbm.at[:, h * half:(h + 1) * half, :],
                                      wbuf.at[h, own_rows], in_sem.at[2 + h])
                for h in range(2)]
    hid_in.start()
    grad_in.start()
    barrier = pltpu.get_barrier_semaphore()

    def greet(device):
        pl.semaphore_signal(barrier, inc=1, device_id=device, device_id_type=MESH)

    greet(x_dev)
    greet(y_dev)
    if paired:
        greet(core_dev)

    @pl.when(z < last)
    def _():
        greet(up_dev)

    @pl.when(z > 0)
    def _():
        greet(down_dev)

    for h in range(2):
        wbuf[h, slots] = jnp.zeros((half, width), wbuf.dtype)
    dmat[row_tiles * col_tiles] = jnp.zeros((width, width), dmat.dtype)

    peers = (3 if paired else 2) + jnp.where(z < last, 1, 0) + jnp.where(z > 0, 1, 0)
    pl.semaphore_wait(barrier, peers)

    sent = []

    def copy(src, dst, send, recv, device):
        return pltpu.make_async_remote_copy(
            src_ref=src, dst_ref=dst, send_sem=send, recv_sem=recv,
            device_id=device, device_id_type=MESH)

    def start(cond, desc):
        if cond is None:
            desc.start()
        else:
            @pl.when(cond)
            def _():
                desc.start()
        sent.append((cond, desc))

    def wait_recv(cond, desc):
        if cond is None:
            desc.wait_recv()
        else:
            @pl.when(cond)
            def _():
                desc.wait_recv()

    def chunk(owner):
        return wbuf.at[group, pl.ds(owner * capacity, capacity)]

    def other_chunk(owner):
        return wbuf.at[1 - group, pl.ds(owner * capacity, capacity)]

    def pick(b):
        return x if b == 0 else 1 - x

    def up_send(j, b):
        part = chunk((z - j) * 2 + pick(b))
        return ((z < last) & (z >= j),
                copy(part, part, ar_sem.at[0, j, b], ar_sem.at[1, j, b], up_dev))

    def up_recv(j, b):
        part = chunk((z - 1 - j) * 2 + pick(b))
        return (z >= j + 1, copy(part, part, ar_sem.at[0, j, b], ar_sem.at[1, j, b], up_dev))

    def down_send(j, b):
        part = chunk((z + j) * 2 + pick(b))
        return ((z > 0) & (z + j <= last),
                copy(part, part, al_sem.at[0, j, b], al_sem.at[1, j, b], down_dev))

    def down_recv(j, b):
        part = chunk((z + 1 + j) * 2 + pick(b))
        return (z + 1 + j <= last,
                copy(part, part, al_sem.at[0, j, b], al_sem.at[1, j, b], down_dev))

    def y_up(j, b, part):
        piece = part((z - 1 - j) * 2 + pick(b))
        return (z >= j + 1, copy(piece, piece, yr_sem.at[0, j, b], yr_sem.at[1, j, b], y_dev))

    def y_down(j, b, part):
        piece = part((z + 1 + j) * 2 + pick(b))
        return (z + 1 + j <= last,
                copy(piece, piece, yl_sem.at[0, j, b], yl_sem.at[1, j, b], y_dev))

    def third(side, owner, sub):
        return wbuf.at[side, pl.ds(owner * capacity + sub * part, part)]

    def y_x(side, sub):
        piece = third(side, z * 2 + 1 - x, sub)
        return copy(piece, piece, yx_sem.at[0, sub], yx_sem.at[1, sub], y_dev)

    mine = store_hbm.at[:, pl.ds(pl.multiple_of(group * half, half), half), :]

    def from_store(cond, sems, device):
        start(cond, copy(mine, chunk(me), sems[0], sems[1], device))

    for sub in range(subs):
        start(None, copy(mine.at[sub * part:(sub + 1) * part], third(group, me, sub),
                         ax_sem.at[0, sub], ax_sem.at[1, sub], x_dev))
    if paired:
        start(None, copy(grad_hbm, gfull.at[core], g_sem.at[0], g_sem.at[1], core_dev))
    from_store(z < last, (ar_sem.at[0, 0, 0], ar_sem.at[1, 0, 0]), up_dev)
    from_store(z > 0, (al_sem.at[0, 0, 0], al_sem.at[1, 0, 0]), down_dev)
    for desc in store_in:
        desc.start()

    def gather_x(sub):
        piece = third(group, z * 2 + 1 - x, sub)
        copy(piece, piece, ax_sem.at[0, sub], ax_sem.at[1, sub], x_dev).wait_recv()
        start(None, y_x(group, sub))
        if sub == subs - 1:
            start(*up_send(0, 1))
            start(*down_send(0, 1))

    hid_in.wait()
    for r in range(row_tiles):
        hid_t[r * width:(r + 1) * width] = hid[:, r * width:(r + 1) * width].T

    pairs = own_tiles // 2

    def columns(side, i):
        return gfull[side, :, pl.ds(pl.multiple_of(2 * i * width, 2 * width), 2 * width)]

    def gradients(side):
        def body(i, carry):
            term = jnp.dot(hid_t[...], columns(side, i), preferred_element_type=jnp.float32)
            term = (term * scale).astype(dmat.dtype)
            at = side * own_tiles + 2 * i
            for r in range(row_tiles):
                for q in range(2):
                    dmat[r * col_tiles + at + q] = term[r * width:(r + 1) * width,
                                                        q * width:(q + 1) * width]
            return carry
        lax.fori_loop(0, pairs, body, 0)

    grad_in.wait()
    gradients(first)
    if paired:
        there = gfull.at[1 - core]
        copy(there, there, g_sem.at[0], g_sem.at[1], core_dev).wait_recv()
        gradients(1 - core)

    def pieces(owner, sub):
        base = owner * capacity + sub * part

        def body(s, carry):
            pbuf[base + s] = dmat[tab[base + s]]
            return carry
        lax.fori_loop(0, part, body, 0, unroll=True)

    def shard(owner, sub):
        return pbuf.at[pl.ds(owner * capacity + sub * part, part)]

    def target(k):
        value = jnp.int32(0)
        for at in range(lines):
            order = sorted(range(lines), key=lambda t: -abs(t - at))
            value = jnp.where(z == at, order[k], value)
        return value

    def gather_z(j, b):
        wait_recv(*up_recv(j, b))
        if j + 1 < last:
            start(*up_send(j + 1, b))
        start(*y_up(j, b, chunk))
        wait_recv(*down_recv(j, b))
        if j + 1 < last:
            start(*down_send(j + 1, b))
        start(*y_down(j, b, chunk))

    steps = [functools.partial(gather_x, sub) for sub in range(subs)]
    for j in range(last):
        for b in range(2):
            steps.append(functools.partial(gather_z, j, b))
    steps = iter(steps)

    def gather_step():
        step = next(steps, None)
        if step is not None:
            step()

    targets = [target(k) for k in range(lines)]

    def x_copy(k, sub):
        owner = targets[k] * 2 + 1 - x
        i = k * subs + sub
        return copy(shard(owner, sub), xrecv.at[i], rx_sem.at[0, i], rx_sem.at[1, i], x_dev)

    for k in range(lines):
        for sub in range(subs):
            pieces(targets[k] * 2 + 1 - x, sub)
            start(None, x_copy(k, sub))
    for k in range(lines):
        for sub in range(subs):
            pieces(targets[k] * 2 + x, sub)
        if k < subs:
            gather_step()

    def arrived(slot, k, sub):
        copy(zrecv.at[slot, sub], zrecv.at[slot, sub], rz_send.at[k, sub],
             rz_recv.at[slot, sub], x_dev).wait_recv()

    def add_up(k, sub):
        goal = targets[k]
        i = k * subs + sub
        base = (goal * 2 + x) * capacity + sub * part
        x_copy(k, sub).wait_recv()
        through = ((goal > z) & (z > 0)) | ((goal < z) & (z < last))

        @pl.when(through)
        def _():
            arrived(goal, k, sub)

            def body(s, carry):
                total = (pbuf[base + s].astype(jnp.float32) + xrecv[i, s].astype(jnp.float32)
                         + zrecv[goal, sub, s].astype(jnp.float32))
                pbuf[base + s] = total.astype(pbuf.dtype)
                return carry
            lax.fori_loop(0, part, body, 0)

        @pl.when(jnp.logical_not(through))
        def _():
            def body(s, carry):
                total = pbuf[base + s].astype(jnp.float32) + xrecv[i, s].astype(jnp.float32)
                pbuf[base + s] = total.astype(pbuf.dtype)
                return carry
            lax.fori_loop(0, part, body, 0)

        source = pbuf.at[pl.ds(base, part)]
        land = jnp.where(goal == z - 1, lines, goal)
        start(goal > z, copy(source, zrecv.at[goal, sub], rz_send.at[k, sub],
                             rz_recv.at[goal, sub], up_dev))
        start(goal < z, copy(source, zrecv.at[land, sub], rz_send.at[k, sub],
                             rz_recv.at[land, sub], down_dev))

    def finish(sub):
        k = last
        i = k * subs + sub
        base = me * capacity + sub * part
        x_copy(k, sub).wait_recv()

        def body(s, carry):
            tg_ref[sub * part + s] = (pbuf[base + s].astype(jnp.float32)
                                      + xrecv[i, s].astype(jnp.float32))
            return carry
        lax.fori_loop(0, part, body, 0)

        for cond, slot in ((z > 0, z), (z < last, lines)):
            @pl.when(cond)
            def _():
                arrived(slot, k, sub)

                def more(s, carry):
                    at = sub * part + s
                    tg_ref[at] = tg_ref[at] + zrecv[slot, sub, s].astype(jnp.float32)
                    return carry
                lax.fori_loop(0, part, more, 0)

    for k in range(last):
        for sub in range(subs):
            gather_step()
            add_up(k, sub)
    for step in steps:
        step()

    for desc in store_in:
        desc.wait()
    for sub in range(subs):
        y_x(1 - group, sub).wait_recv()
    for j in range(last):
        for b in range(2):
            wait_recv(*y_up(j, b, other_chunk))
            wait_recv(*y_down(j, b, other_chunk))

    gh_acc[...] = jnp.zeros_like(gh_acc)

    def products(side, i):
        c0 = side * own_tiles + 2 * i
        for r in range(row_tiles):
            for q in range(2):
                at = tab[slots + r * col_tiles + c0 + q]
                for h in range(2):
                    block[r * width + h * half:r * width + (h + 1) * half,
                          q * width:(q + 1) * width] = wbuf[h, at]
        dense = block[...]
        cot = columns(side, i)
        gh_acc[...] += lax.dot_general(cot, dense, (((1,), (1,)), ((), ())),
                                       preferred_element_type=jnp.float32)
        out = jnp.dot(hid[...], dense, preferred_element_type=jnp.float32)
        return out.astype(jnp.bfloat16)

    if paired:
        def partial_copy(i):
            return copy(psend.at[i], precv.at[i], p_sem.at[0, i], p_sem.at[1, i], core_dev)

        def away(i, carry):
            psend[i] = products(1 - core, i)
            partial_copy(i).start()
            return carry
        lax.fori_loop(0, pairs, away, 0)

        def home(i, carry):
            pown[i] = products(core, i)
            return carry
        lax.fori_loop(0, pairs, home, 0)
        gh_ref[...] = gh_acc[...].astype(gh_ref.dtype)
        for i in range(pairs):
            partial_copy(i).wait()
            mixed_ref[:, 2 * i * width:2 * (i + 1) * width] = (
                pown[i].astype(jnp.float32) + precv[i].astype(jnp.float32)
            ).astype(mixed_ref.dtype)
    else:
        for i in range(pairs):
            mixed_ref[:, 2 * i * width:2 * (i + 1) * width] = products(0, i)
        gh_ref[...] = gh_acc[...].astype(gh_ref.dtype)

    for sub in range(subs):
        finish(sub)
    for cond, desc in sent:
        if cond is None:
            desc.wait_send()
        else:
            pl.when(cond)(desc.wait_send)


def shards(hidden, grad_out, tile_cols, tile_owner, tile_store):
    owners = lax.axis_size("fsdp")
    paired = lax.axis_size("tensor") == 2
    tokens = hidden.shape[0]
    row_tiles, keep = tile_cols.shape
    capacity, width = tile_store.shape[2:4]
    col_tiles = 2 * keep
    lines = owners // 2
    half = width // 2
    slots = owners * capacity
    scale = float(tokens * owners) ** (-0.5)
    tables = index_tables(tile_cols, tile_owner, owners, capacity, col_tiles)
    if not paired:
        grad_out = lax.all_gather(grad_out, "tensor", axis=1, tiled=True)
    store = tile_store.reshape(capacity, width, width)
    hops = lines - 1
    pairs = grad_out.shape[1] // width // 2
    subs = 3 if capacity % 3 == 0 else 1
    part = capacity // subs
    sides = 2 if paired else 1
    few = pairs if paired else 1
    bf16, f32 = jnp.bfloat16, jnp.float32
    dma = pltpu.SemaphoreType.DMA
    vmem = pl.BlockSpec(memory_space=pltpu.VMEM)
    cfg = (lines, capacity, row_tiles, col_tiles, width, scale, paired, subs)
    mixed, gh, tg = pl.pallas_call(
        functools.partial(kernel, cfg),
        out_shape=(
            jax.ShapeDtypeStruct(grad_out.shape, bf16),
            jax.ShapeDtypeStruct(hidden.shape, bf16),
            jax.ShapeDtypeStruct((capacity, width, width), f32),
        ),
        in_specs=[pl.BlockSpec(memory_space=pltpu.SMEM)] + [pl.BlockSpec(memory_space=pl.ANY)] * 3,
        out_specs=(vmem,) * 3,
        scratch_shapes=[
            pltpu.VMEM(hidden.shape, bf16),
            pltpu.VMEM((row_tiles * width, tokens), bf16),
            pltpu.VMEM((sides,) + grad_out.shape, bf16),
            pltpu.VMEM((2, slots + 1, half, width), bf16),
            pltpu.VMEM((row_tiles * col_tiles + 1, width, width), bf16),
            pltpu.VMEM((slots, width, width), bf16),
            pltpu.VMEM((lines * subs, part, width, width), bf16),
            pltpu.VMEM((lines + 1, subs, part, width, width), bf16),
            pltpu.VMEM((row_tiles * width, 2 * width), bf16),
            pltpu.VMEM(hidden.shape, f32),
            pltpu.VMEM((few, tokens, 2 * width), bf16),
            pltpu.VMEM((few, tokens, 2 * width), bf16),
            pltpu.VMEM((few, tokens, 2 * width), bf16),
            dma((4,)), dma((2,)), dma((2, subs)), dma((2, hops, 2)), dma((2, hops, 2)),
            dma((2, subs)), dma((2, hops, 2)), dma((2, hops, 2)),
            dma((2, lines * subs)), dma((lines, subs)), dma((lines + 1, subs)), dma((2, few)),
        ],
        compiler_params=pltpu.CompilerParams(
            collective_id=0, has_side_effects=True, vmem_limit_bytes=56 * 1024 * 1024),
    )(tables, hidden, grad_out, store)
    if not paired:
        mixed = lax.psum_scatter(mixed, "tensor", scatter_dimension=1, tiled=True)
    return mixed, gh, tg.reshape(1, 1, capacity, width, width)


def solution(mesh):
    placed = (
        P(("groups", "fsdp"), "tensor"),
        P(("groups", "fsdp"), "tensor"),
        P("tensor", None),
        P("tensor", None),
        P("tensor", "fsdp", None, None, None),
    )
    return jax.shard_map(
        shards,
        mesh=mesh,
        in_specs=placed,
        out_specs=(
            P(("groups", "fsdp"), "tensor"),
            P(("groups", "fsdp"), "tensor"),
            P(("groups", "tensor"), "fsdp", None, None, None),
        ),
        check_vma=False,
    )
```
